32 devices in a mesh: node: 4 (over x, core), wide: 8 (over z, y).
Axes of the slice: x: 2, y: 2, z: 4, core: 2. Of those that a mesh axis runs over, the one named last changes fastest.
Arguments:
- tokens: bfloat16 [2048, 4096], P(('node', 'wide')), may hold values from -6 to 6
- expert_ids: int32 [2048, 6], P(('node', 'wide')), may hold values from 0 to 31, all different within a row; in each aligned block of 64 rows (0 to 63, 64 to 127, ...) at most 16 rows name the same one
- gate_weights: float32 [2048, 6], P(('node', 'wide')), may hold values from 0.1 to 1
- w_gate: bfloat16 [32, 4096, 768], P(('node', 'wide')), may hold values from -0.09375 to 0.09375
- w_up: bfloat16 [32, 4096, 768], P(('node', 'wide')), may hold values from -0.09375 to 0.09375
- w_down: bfloat16 [32, 768, 4096], P(('node', 'wide')), may hold values from -0.21875 to 0.21875
- gate_scale: float32 [32, 768], P(('node', 'wide')), may hold values from 0.5 to 2
- up_scale: float32 [32, 768], P(('node', 'wide')), may hold values from 0.5 to 2
- down_scale: float32 [32, 4096], P(('node', 'wide')), may hold values from 0.5 to 2
Outputs:
- mixed: bfloat16 [2048, 4096], P(('node', 'wide'))
The draws below stay inside these ranges and needn't reach their ends.
Inputs may be any that keep to these rules, and one draw needn't show every extreme that they name: `expert_ids`: each token names 6 different experts; among the routes of the tokens of one device no expert is named more than 16 times, a bound that some block reaches.
All inputs are finite; a program needn't handle non-finite values.
Results may differ from the reference program's by a relative error of at most 0.0058.
Values may be sent and summed in bfloat16 or wider, within the bound.
A program may use at most 128 MiB of HBM per device.

```python
import math
import jax
import jax.numpy as jnp
import numpy as np
from jax import lax

D = 4096
TOP = 6
FFW = 768
TOK_DEV = 64
EXPERTS = 32
TOKENS = 2048
CAP = 16


def block_levels(stream_key, dims, cuts, smallest, largest):
    def one(dim, parts):
        draws = jax.random.uniform(jax.random.fold_in(jax.random.fold_in(stream_key, 6), dim), (parts,), jnp.float32, smallest / len(cuts), largest / len(cuts))
        return jnp.repeat(jnp.exp(draws), dims[dim] // parts).reshape((-1,) + (1,) * (len(dims) - dim - 1))

    loudness = one(*cuts[0])
    for cut in cuts[1:]:
        loudness = loudness * one(*cut)
    return loudness


def assign_block(key, own, number, rows, amount, top, most, slope):
    order = jax.random.permutation(key, amount)
    packed, ordinary = load_shares(amount, rows * top, most, slope, True), load_shares(amount, rows * top, most, slope, False)
    places = jnp.arange(amount)

    def named(tallies, offset_by):
        used = int((tallies > 0).sum())
        fixed = max(1, used // 4)
        shifted = fixed + (places - fixed + offset_by * (used - fixed)) % max(1, amount - fixed)
        return jnp.zeros((amount,), jnp.int32).at[order[jnp.where(places < fixed, places, shifted)]].set(jnp.asarray(tallies, jnp.int32))

    tallies = jnp.where(number % 4 == 0, named(packed, number // 4), named(ordinary, number - number // 4 - 1))
    mixed = jax.random.permutation(jax.random.fold_in(own, 3), amount)
    source_of, taker = mixed[0:amount // 2 * 2:2], mixed[1:amount // 2 * 2:2]
    margin = jnp.minimum(tallies[source_of] - 1, most - tallies[taker]) // 2
    margin = jnp.where((source_of == order[0]) | (taker == order[0]) | (tallies[taker] == 0), 0, jnp.maximum(margin, 0))
    shifted = jax.random.randint(jax.random.fold_in(own, 4), (amount // 2,), 0, 1 << 20) % (margin + 1)
    tallies = tallies.at[source_of].add(-shifted).at[taker].add(shifted)
    labels = jnp.searchsorted(jnp.cumsum(tallies), jnp.arange(rows * top), side="right").astype(jnp.int32)
    grid = labels.reshape(top, rows).T
    grid = grid[jax.random.permutation(jax.random.fold_in(own, 1), rows)]
    offset_by = jax.random.randint(jax.random.fold_in(own, 2), (rows, 1), 0, top)
    return jnp.take_along_axis(grid, (jnp.arange(top)[None, :] + offset_by) % top, axis=1)


def load_shares(number_of, total, most, slope, full):
    weights = [(1 << 20) // math.isqrt(grade ** slope) + 1 for grade in range(1, number_of + 1)]
    largest = most if full else min(most, max(-(-total // number_of), total * weights[0] // sum(weights)))
    least = 1 if total - largest >= number_of - 1 else 0
    counts, surplus = [largest] + [least] * (number_of - 1), total - largest - least * (number_of - 1)
    while surplus > 0:
        free = [i for i in range(1, number_of) if counts[i] < largest] or [i for i in range(1, number_of) if counts[i] < most]
        pool, left = sum([weights[i] for i in free]), surplus
        for i in free:
            addition = min(most - counts[i], max(1, left * weights[i] // pool), surplus)
            counts[i] = counts[i] + addition
            surplus = surplus - addition
    return np.array(counts)


def centred(own_key, dims, deviation, most, pieces=(), kind=jnp.bfloat16):
    level = block_levels(own_key, dims, pieces, -0.22, 0.18) if pieces else 1.0
    values = jax.random.normal(own_key, dims, jnp.float32) * deviation * level
    return jnp.minimum(jnp.maximum(values, -most), most).astype(kind)


def setup_inputs(seed: int = 0) -> dict:
    key_of = jax.random.split(jax.random.key(seed), 10)
    tokens = centred(key_of[0], (TOKENS, D), 1.0, 6.0, ((0, 32),))
    expert_ids_keys = jax.random.split(jax.random.fold_in(key_of[1], 1), TOKENS // TOK_DEV)
    expert_ids_turns = jax.random.permutation(jax.random.fold_in(key_of[1], 3), TOKENS // TOK_DEV)
    expert_ids = jax.vmap(lambda own, number: assign_block(jax.random.fold_in(key_of[1], 2), own, number, TOK_DEV, EXPERTS, TOP, CAP, 2))(expert_ids_keys, expert_ids_turns).reshape((TOKENS, TOP))
    gate_weights = jnp.clip(0.1 + 0.9 * jax.random.uniform(key_of[2], (TOKENS, TOP), jnp.float32) ** block_levels(key_of[2], (TOKENS, TOP), ((0, 32),), -0.2, 0.2), 0.1, 1.0)
    w_gate = centred(key_of[3], (EXPERTS, D, FFW), D ** -0.5, 0.09375, ((0, 32),))
    w_up = centred(key_of[4], (EXPERTS, D, FFW), D ** -0.5, 0.09375, ((0, 32),))
    w_down = centred(key_of[5], (EXPERTS, FFW, D), FFW ** -0.5, 0.21875, ((0, 32),))
    gate_scale = jnp.clip(jnp.exp(math.log(2.0) - 1.3862944 * jax.random.uniform(key_of[6], (EXPERTS, FFW), jnp.float32) ** block_levels(key_of[6], (EXPERTS, FFW), ((0, 32),), -0.2, 0.2)), 0.5, 2.0)
    up_scale = jnp.clip(jnp.exp(math.log(2.0) - 1.3862944 * jax.random.uniform(key_of[7], (EXPERTS, FFW), jnp.float32) ** block_levels(key_of[7], (EXPERTS, FFW), ((0, 32),), -0.2, 0.2)), 0.5, 2.0)
    down_scale = jnp.clip(jnp.exp(math.log(2.0) - 1.3862944 * jax.random.uniform(key_of[8], (EXPERTS, D), jnp.float32) ** block_levels(key_of[8], (EXPERTS, D), ((0, 32),), -0.2, 0.2)), 0.5, 2.0)
    return dict(tokens=tokens, expert_ids=expert_ids, gate_weights=gate_weights, w_gate=w_gate, w_up=w_up, w_down=w_down, gate_scale=gate_scale, up_scale=up_scale, down_scale=down_scale)


def reference(tokens, expert_ids, gate_weights, w_gate, w_up, w_down, gate_scale, up_scale, down_scale):
    blocks = TOKENS // TOK_DEV
    block_ids = expert_ids.reshape(blocks, TOK_DEV * TOP)
    onehot = (block_ids[:, :, None] == jnp.arange(EXPERTS, dtype=jnp.int32)[None, None, :]).astype(jnp.int32)
    before = jnp.cumsum(onehot, axis=1) - onehot
    position = jnp.sum(before * onehot, axis=2).astype(jnp.int32)
    slot_rows = (jnp.arange(blocks, dtype=jnp.int32)[:, None] * CAP + position).reshape(-1).astype(jnp.int32)
    flat_ids = expert_ids.reshape(-1).astype(jnp.int32)
    token_of = (jnp.arange(TOKENS * TOP, dtype=jnp.int32) // TOP).astype(jnp.int32)
    table = jnp.full((EXPERTS, blocks * CAP), TOKENS, jnp.int32).at[flat_ids, slot_rows].set(token_of)
    weight_of = jnp.zeros((EXPERTS, blocks * CAP), jnp.float32).at[flat_ids, slot_rows].set(gate_weights.reshape(-1))
    padded = jnp.concatenate([tokens, jnp.zeros((1, D), jnp.bfloat16)], axis=0)

    def one_expert(total, inputs):
        index, weight, g_mat, u_mat, d_mat, g_scale, u_scale, d_scale = inputs
        rows = padded[index]
        gate = jnp.dot(rows, g_mat, preferred_element_type=jnp.float32) * g_scale
        up = jnp.dot(rows, u_mat, preferred_element_type=jnp.float32) * u_scale
        hidden = (jax.nn.silu(gate) * up).astype(jnp.bfloat16)
        routed = (jnp.dot(hidden, d_mat, preferred_element_type=jnp.float32) * d_scale).astype(jnp.bfloat16)
        total = total.at[index].add(weight[:, None] * routed.astype(jnp.float32), mode="drop")
        return total, None

    start = jnp.zeros((TOKENS, D), jnp.float32)
    total, unused = lax.scan(one_expert, start, (table, weight_of, w_gate, w_up, w_down, gate_scale, up_scale, down_scale))
    return total.astype(jnp.bfloat16)
```

```python
import functools
import math

import jax
import jax.numpy as jnp
from jax import lax
from jax.experimental import pallas as pl
from jax.experimental.pallas import tpu as pltpu
from jax.sharding import PartitionSpec as P

MESH = pl.DeviceIdType.MESH
CHUNKS = 8
LAG = 1


def tile_of(size, most):
    return most if size % most == 0 else size


def kernel(
    groups,
    ring,
    tok_ref,
    meta_ref,
    gate_hbm,
    up_hbm,
    down_hbm,
    gate_scale_ref,
    up_scale_ref,
    down_scale_ref,
    out_ref,
    metas,
    tokens,
    packed,
    rows,
    w_gate,
    w_up,
    w_down,
    gate,
    up,
    hidden,
    results,
    returned,
    partial,
    partials,
    dispatch,
    weighted,
    combine,
    meta_sems,
    weight_sems,
    out_z,
    in_z,
    own_z,
    out_p,
    in_p,
    own_p,
    back_out_p,
    back_in_p,
    back_own_p,
    back_out_z,
    back_in_z,
    back_own_z,
):
    chunks, _, cols = tokens.shape
    count = tok_ref.shape[0]
    members = metas.shape[1] // 2
    slots = packed.shape[1] // members
    node, wide = lax.axis_index("node"), lax.axis_index("wide")
    my_group, my_ring = lax.div(wide, ring), lax.rem(wide, ring)
    me = node * ring + my_ring

    def group_at(i):
        return lax.rem(my_group + i, groups)

    def group_id(g):
        return (node, g * ring + my_ring)

    def member_at(i):
        return lax.rem(me + i, members)

    def member_id(d):
        return (lax.div(d, ring), my_group * ring + lax.rem(d, ring))

    def part(index, size):
        return pl.ds(pl.multiple_of(index * size, size), size)

    def arrived(ref, sem):
        pltpu.make_async_copy(ref, ref, sem).wait()

    weights = [
        pltpu.make_async_copy(gate_hbm.at[0], w_gate, weight_sems.at[0]),
        pltpu.make_async_copy(up_hbm.at[0], w_up, weight_sems.at[1]),
        pltpu.make_async_copy(down_hbm.at[0], w_down, weight_sems.at[2]),
    ]

    barrier = pltpu.get_barrier_semaphore()

    @pl.loop(1, groups)
    def _(i):
        pl.semaphore_signal(barrier, inc=1, device_id=group_id(group_at(i)), device_id_type=MESH)

    @pl.loop(1, members)
    def _(i):
        pl.semaphore_signal(barrier, inc=1, device_id=member_id(member_at(i)), device_id_type=MESH)

    for w in weights:
        w.start()
    pl.semaphore_wait(barrier, groups + members - 2)

    @pl.loop(1, groups)
    def _(i):
        g = group_at(i)
        pltpu.make_async_remote_copy(
            src_ref=meta_ref.at[g],
            dst_ref=metas.at[my_group],
            send_sem=meta_sems.at[0],
            recv_sem=meta_sems.at[1],
            device_id=group_id(g),
            device_id_type=MESH,
        ).start()

    @pl.loop(0, chunks)
    def _(c):
        mine = tok_ref.at[:, part(c, cols)]
        place = tokens.at[c, part(my_group, count)]

        @pl.loop(1, groups)
        def _(i):
            pltpu.make_async_remote_copy(
                src_ref=mine,
                dst_ref=place,
                send_sem=out_z.at[c],
                recv_sem=in_z.at[c],
                device_id=group_id(group_at(i)),
                device_id_type=MESH,
            ).start()

        pltpu.make_async_copy(mine, place, own_z.at[c]).start()

    gate[...] = jnp.zeros_like(gate)
    up[...] = jnp.zeros_like(up)

    own_meta = pltpu.make_async_copy(meta_ref.at[my_group], metas.at[my_group], meta_sems.at[2])
    own_meta.start()
    own_meta.wait()
    arrived(metas.at[pl.ds(0, groups - 1)], meta_sems.at[1])
    place = jnp.max(metas[:, :members, :], axis=0)
    weight = jnp.sum(metas[:, members:, :], axis=0)
    slot = lax.broadcasted_iota(jnp.int32, (slots, groups * count), 0).astype(jnp.float32)
    for d in range(members):
        same = place[d : d + 1, :] == slot
        dispatch[pl.ds(d * slots, slots), :] = jnp.where(same, 1.0, 0.0).astype(jnp.bfloat16)
        weighted[pl.ds(d * slots, slots), :] = jnp.where(same, weight[d : d + 1, :], 0.0)
    combine[...] = weighted[...].T.astype(jnp.bfloat16)

    half = tile_of(cols, 256)

    def pack(c):
        pltpu.make_async_copy(
            tok_ref.at[:, part(c, cols)], tokens.at[c, part(my_group, count)], own_z.at[c]
        ).wait()
        arrived(tokens.at[c, pl.ds(0, (groups - 1) * count)], in_z.at[c])

        @pl.loop(0, cols // half)
        def _(j):
            packed[c, :, part(j, half)] = jnp.dot(
                dispatch[...], tokens[c, :, part(j, half)], preferred_element_type=jnp.float32
            ).astype(jnp.bfloat16)

        @pl.loop(1, members)
        def _(i):
            d = member_at(i)
            pltpu.make_async_remote_copy(
                src_ref=packed.at[c, part(d, slots)],
                dst_ref=rows.at[c, part(me, slots)],
                send_sem=out_p.at[c],
                recv_sem=in_p.at[c],
                device_id=member_id(d),
                device_id_type=MESH,
            ).start()

        pltpu.make_async_copy(
            packed.at[c, part(me, slots)], rows.at[c, part(me, slots)], own_p.at[c]
        ).start()

    wide_tile = tile_of(gate.shape[1], 256)

    def project(c):
        pltpu.make_async_copy(
            packed.at[c, part(me, slots)], rows.at[c, part(me, slots)], own_p.at[c]
        ).wait()
        arrived(rows.at[c, pl.ds(0, (members - 1) * slots)], in_p.at[c])

        @pl.loop(0, gate.shape[1] // wide_tile)
        def _(j):
            at = part(j, wide_tile)
            gate[:, at] += jnp.dot(
                rows[c], w_gate[part(c, cols), at], preferred_element_type=jnp.float32
            )
            up[:, at] += jnp.dot(
                rows[c], w_up[part(c, cols), at], preferred_element_type=jnp.float32
            )

    @pl.loop(0, LAG)
    def _(c):
        pack(c)

    weights[0].wait()
    weights[1].wait()

    @pl.loop(LAG, chunks)
    def _(c):
        pack(c)
        project(c - LAG)

    weights[2].wait()

    @pl.loop(chunks - LAG, chunks)
    def _(c):
        project(c)

    @pl.loop(0, gate.shape[1] // wide_tile)
    def _(j):
        at = part(j, wide_tile)
        g = gate[:, at] * gate_scale_ref[:, at]
        hidden[:, at] = (g / (1.0 + jnp.exp(-g)) * (up[:, at] * up_scale_ref[:, at])).astype(jnp.bfloat16)

    @pl.loop(0, chunks)
    def _(c):
        @pl.loop(0, cols // half)
        def _(j):
            at = part(c * (cols // half) + j, half)
            results[c, :, part(j, half)] = (
                jnp.dot(hidden[...], w_down[:, at], preferred_element_type=jnp.float32)
                * down_scale_ref[:, at]
            ).astype(jnp.bfloat16)

        @pl.loop(1, members)
        def _(i):
            d = member_at(i)
            pltpu.make_async_remote_copy(
                src_ref=results.at[c, part(d, slots)],
                dst_ref=returned.at[c, part(me, slots)],
                send_sem=back_out_p.at[c],
                recv_sem=back_in_p.at[c],
                device_id=member_id(d),
                device_id_type=MESH,
            ).start()

        pltpu.make_async_copy(
            results.at[c, part(me, slots)], returned.at[c, part(me, slots)], back_own_p.at[c]
        ).start()

    @pl.loop(0, chunks)
    def _(c):
        pltpu.make_async_copy(
            results.at[c, part(me, slots)], returned.at[c, part(me, slots)], back_own_p.at[c]
        ).wait()
        arrived(returned.at[c, pl.ds(0, (members - 1) * slots)], back_in_p.at[c])

        @pl.loop(0, cols // half)
        def _(j):
            partial[c, :, part(j, half)] = jnp.dot(
                combine[...], returned[c, :, part(j, half)], preferred_element_type=jnp.float32
            ).astype(jnp.bfloat16)

        @pl.loop(1, groups)
        def _(i):
            g = group_at(i)
            pltpu.make_async_remote_copy(
                src_ref=partial.at[c, part(g, count)],
                dst_ref=partials.at[c, part(my_group, count)],
                send_sem=back_out_z.at[c],
                recv_sem=back_in_z.at[c],
                device_id=group_id(g),
                device_id_type=MESH,
            ).start()

        pltpu.make_async_copy(
            partial.at[c, part(my_group, count)],
            partials.at[c, part(my_group, count)],
            back_own_z.at[c],
        ).start()

    @pl.loop(0, chunks)
    def _(c):
        pltpu.make_async_copy(
            partial.at[c, part(my_group, count)],
            partials.at[c, part(my_group, count)],
            back_own_z.at[c],
        ).wait()
        arrived(partials.at[c, pl.ds(0, (groups - 1) * count)], back_in_z.at[c])
        total = partials[c, pl.ds(0, count), :].astype(jnp.float32)
        for g in range(1, groups):
            total += partials[c, pl.ds(g * count, count), :].astype(jnp.float32)
        out_ref[:, part(c, cols)] = total.astype(jnp.bfloat16)

    arrived(metas.at[pl.ds(0, groups - 1)], meta_sems.at[0])

    @pl.loop(0, chunks)
    def _(c):
        arrived(tokens.at[c, pl.ds(0, (groups - 1) * count)], out_z.at[c])
        arrived(packed.at[c, pl.ds(0, (members - 1) * slots)], out_p.at[c])
        arrived(results.at[c, pl.ds(0, (members - 1) * slots)], back_out_p.at[c])
        arrived(partial.at[c, pl.ds(0, (groups - 1) * count)], back_out_z.at[c])


def on_device(
    tokens, expert_ids, gate_weights, w_gate, w_up, w_down, gate_scale, up_scale, down_scale
):
    count, top = expert_ids.shape
    width = tokens.shape[1]
    inner = w_gate.shape[2]
    nodes, wides = lax.axis_size("node"), lax.axis_size("wide")
    experts = nodes * wides
    capacity = max(2, 4 * count * top // (3 * experts))
    groups = math.gcd(4, wides)
    ring = wides // groups
    members = nodes * ring
    slots = groups * capacity
    held = groups * count
    chunks = CHUNKS
    cols = width // chunks

    my_group = lax.axis_index("wide") // ring
    named = expert_ids.T[:, None, :] == jnp.arange(experts, dtype=jnp.int32)[None, :, None]
    picked = jnp.any(named, axis=0)
    weight = jnp.sum(jnp.where(named, gate_weights.T[:, None, :], 0.0), axis=0)
    earlier = jnp.arange(count)[:, None] < jnp.arange(count)[None, :]
    position = jnp.dot(
        picked.astype(jnp.bfloat16), earlier.astype(jnp.bfloat16), preferred_element_type=jnp.float32
    )
    place = jnp.where(picked, position + (my_group * capacity).astype(jnp.float32), -1.0)
    here = (jnp.arange(held) // count == my_group)[None, :]
    place = jnp.where(here, jnp.tile(place, (1, groups)), -1.0)
    weight = jnp.where(here, jnp.tile(weight, (1, groups)), 0.0)
    meta = jnp.stack([place, weight]).reshape(2, nodes, groups, ring, held)
    meta = meta.transpose(2, 0, 1, 3, 4).reshape(groups, 2 * members, held)

    vmem = pl.BlockSpec(memory_space=pltpu.VMEM)
    anywhere = pl.BlockSpec(memory_space=pl.ANY)
    rows = members * slots
    bf16, f32 = jnp.bfloat16, jnp.float32
    per_chunk = pltpu.SemaphoreType.DMA((chunks,))
    return pl.pallas_call(
        functools.partial(kernel, groups, ring),
        out_shape=jax.ShapeDtypeStruct((count, width), bf16),
        in_specs=[vmem, vmem, anywhere, anywhere, anywhere, vmem, vmem, vmem],
        out_specs=vmem,
        scratch_shapes=[
            pltpu.VMEM((groups, 2 * members, held), f32),
            pltpu.VMEM((chunks, held, cols), bf16),
            pltpu.VMEM((chunks, rows, cols), bf16),
            pltpu.VMEM((chunks, rows, cols), bf16),
            pltpu.VMEM((width, inner), bf16),
            pltpu.VMEM((width, inner), bf16),
            pltpu.VMEM((inner, width), bf16),
            pltpu.VMEM((rows, inner), f32),
            pltpu.VMEM((rows, inner), f32),
            pltpu.VMEM((rows, inner), bf16),
            pltpu.VMEM((chunks, rows, cols), bf16),
            pltpu.VMEM((chunks, rows, cols), bf16),
            pltpu.VMEM((chunks, held, cols), bf16),
            pltpu.VMEM((chunks, held, cols), bf16),
            pltpu.VMEM((rows, held), bf16),
            pltpu.VMEM((rows, held), f32),
            pltpu.VMEM((held, rows), bf16),
            pltpu.SemaphoreType.DMA((3,)),
            pltpu.SemaphoreType.DMA((3,)),
        ]
        + [per_chunk] * 12,
        compiler_params=pltpu.CompilerParams(
            collective_id=0, has_side_effects=True, vmem_limit_bytes=60 * 2**20
        ),
    )(tokens, meta, w_gate, w_up, w_down, gate_scale, up_scale, down_scale)


def solution(mesh):
    placed = (
        P(("node", "wide"), None),
        P(("node", "wide"), None),
        P(("node", "wide"), None),
        P(("node", "wide"), None, None),
        P(("node", "wide"), None, None),
        P(("node", "wide"), None, None),
        P(("node", "wide"), None),
        P(("node", "wide"), None),
        P(("node", "wide"), None),
    )
    return jax.shard_map(
        on_device, mesh=mesh, in_specs=placed, out_specs=P(("node", "wide"), None), check_vma=False
    )
```

```python
import functools
import math

import jax
import jax.numpy as jnp
from jax import lax
from jax.experimental import pallas as pl
from jax.experimental.pallas import tpu as pltpu
from jax.sharding import PartitionSpec as P

MESH = pl.DeviceIdType.MESH
CHUNKS = 8
LAG = 1


def tile_of(size, most):
    return most if size % most == 0 else size


def kernel(
    groups,
    ring,
    early,
    tok_ref,
    meta_ref,
    gate_hbm,
    up_hbm,
    down_hbm,
    gate_scale_ref,
    up_scale_ref,
    down_scale_ref,
    out_ref,
    metas,
    tokens,
    packed,
    rows,
    w_gate,
    w_up,
    w_down,
    gate,
    up,
    hidden,
    results,
    returned,
    partial,
    partials,
    dispatch,
    weighted,
    combine,
    meta_sems,
    weight_sems,
    out_z,
    in_z,
    own_z,
    out_p,
    in_p,
    own_p,
    early_out_p,
    early_in_p,
    relay_z,
    back_out_p,
    back_in_p,
    back_own_p,
    late_out_p,
    late_in_p,
    late_own_p,
    back_out_z,
    back_in_z,
):
    chunks, _, cols = tokens.shape
    count = tok_ref.shape[0]
    members = metas.shape[1] // 2
    first = members * early
    slots = packed.shape[1] // members - early
    away = 1 if early else 0
    held = groups * count
    node, wide = lax.axis_index("node"), lax.axis_index("wide")
    my_group, my_ring = lax.div(wide, ring), lax.rem(wide, ring)
    me = node * ring + my_ring

    is_end = jnp.logical_or(my_group == 0, my_group == groups - 1)
    relays = groups == 4

    def group_at(i):
        return lax.rem(my_group + i, groups)

    def group_id(g):
        return (node, g * ring + my_ring)

    def member_at(i):
        return lax.rem(me + i, members)

    def member_id(d):
        return (lax.div(d, ring), my_group * ring + lax.rem(d, ring))

    def part(index, size):
        return pl.ds(pl.multiple_of(index * size, size), size)

    def arrived(ref, sem):
        pltpu.make_async_copy(ref, ref, sem).wait()

    weights = [
        pltpu.make_async_copy(gate_hbm.at[0], w_gate, weight_sems.at[0]),
        pltpu.make_async_copy(up_hbm.at[0], w_up, weight_sems.at[1]),
        pltpu.make_async_copy(down_hbm.at[0], w_down, weight_sems.at[2]),
    ]

    barrier = pltpu.get_barrier_semaphore()

    @pl.loop(1, groups)
    def _(i):
        pl.semaphore_signal(barrier, inc=1, device_id=group_id(group_at(i)), device_id_type=MESH)

    @pl.loop(1, members)
    def _(i):
        pl.semaphore_signal(barrier, inc=1, device_id=member_id(member_at(i)), device_id_type=MESH)

    for w in weights:
        w.start()
    pl.semaphore_wait(barrier, groups + members - 2)

    half = tile_of(cols, 256)

    @pl.loop(1, groups)
    def _(i):
        g = group_at(i)
        pltpu.make_async_remote_copy(
            src_ref=meta_ref.at[g],
            dst_ref=metas.at[groups - i],
            send_sem=meta_sems.at[0],
            recv_sem=meta_sems.at[1],
            device_id=group_id(g),
            device_id_type=MESH,
        ).start()

    @pl.loop(0, chunks)
    def _(c):
        mine = tok_ref.at[:, part(c, cols)]

        @pl.loop(1, groups)
        def _(i):
            g = group_at(i)
            direct = jnp.logical_not(jnp.logical_and(is_end, my_group + g == groups - 1))

            @pl.when(jnp.logical_or(direct, not relays))
            def _():
                pltpu.make_async_remote_copy(
                    src_ref=mine,
                    dst_ref=tokens.at[c, part(groups - i, count)],
                    send_sem=out_z.at[c],
                    recv_sem=in_z.at[c],
                    device_id=group_id(g),
                    device_id_type=MESH,
                ).start()

        pltpu.make_async_copy(mine, tokens.at[c, pl.ds(0, count)], own_z.at[c]).start()

    def fill(place, weight, at, base, size):
        slot = base + lax.broadcasted_iota(jnp.int32, (size, held), 0).astype(jnp.float32)
        for d in range(members):
            same = place[d : d + 1, :] == slot
            dispatch[pl.ds(at + d * size, size), :] = jnp.where(same, 1.0, 0.0).astype(jnp.bfloat16)
            weighted[pl.ds(at + d * size, size), :] = jnp.where(same, weight[d : d + 1, :], 0.0)

    metas[0] = meta_ref[my_group]
    if early:
        fill(metas[0, :members, :], metas[0, members:, :], 0, 0.0, early)

        @pl.loop(0, chunks)
        def _(c):
            @pl.loop(0, cols // half)
            def _(j):
                packed[c, pl.ds(0, first), part(j, half)] = jnp.dot(
                    dispatch[pl.ds(0, first), pl.ds(0, count)],
                    tok_ref[:, part(c * (cols // half) + j, half)],
                    preferred_element_type=jnp.float32,
                ).astype(jnp.bfloat16)

            @pl.loop(1, members)
            def _(i):
                d = member_at(i)
                pltpu.make_async_remote_copy(
                    src_ref=packed.at[c, part(d, early)],
                    dst_ref=rows.at[c, part(me, early)],
                    send_sem=early_out_p.at[c],
                    recv_sem=early_in_p.at[c],
                    device_id=member_id(d),
                    device_id_type=MESH,
                ).start()

    gate[...] = jnp.zeros_like(gate)
    up[...] = jnp.zeros_like(up)

    arrived(metas.at[pl.ds(1, groups - 1)], meta_sems.at[1])
    fill(
        jnp.max(metas[:, :members, :], axis=0),
        jnp.sum(metas[:, members:, :], axis=0),
        first,
        float(early),
        slots,
    )
    combine[...] = weighted[...].T.astype(jnp.bfloat16)

    def rest(d):
        return pl.ds(pl.multiple_of(first + d * slots, early or slots), slots)

    def all_but_one(ref):
        return ref.at[pl.ds(first, (members - 1) * slots)]

    def early_but_one(ref):
        return ref.at[pl.ds(0, (members - 1) * early)]

    def pack(c):
        pltpu.make_async_copy(
            tok_ref.at[:, part(c, cols)], tokens.at[c, pl.ds(0, count)], own_z.at[c]
        ).wait()
        arrived(tokens.at[c, pl.ds(count, (groups - 1) * count)], in_z.at[c])

        if relays:
            @pl.when(jnp.logical_not(is_end))
            def _():
                target = (groups - 1) * (my_group - 1)
                distance = lax.rem(2 * groups - 1 - 2 * target, groups)
                pltpu.make_async_remote_copy(
                    src_ref=tokens.at[c, pl.ds(2 * count, count)],
                    dst_ref=tokens.at[c, part(distance, count)],
                    send_sem=relay_z.at[c],
                    recv_sem=in_z.at[c],
                    device_id=group_id(target),
                    device_id_type=MESH,
                ).start()

        @pl.loop(0, cols // half)
        def _(j):
            packed[c, pl.ds(first, members * slots), part(j, half)] = jnp.dot(
                dispatch[pl.ds(first, members * slots), :],
                tokens[c, :, part(j, half)],
                preferred_element_type=jnp.float32,
            ).astype(jnp.bfloat16)

        @pl.loop(1, members)
        def _(i):
            d = member_at(i)
            pltpu.make_async_remote_copy(
                src_ref=packed.at[c, rest(d)],
                dst_ref=rows.at[c, rest(me)],
                send_sem=out_p.at[c],
                recv_sem=in_p.at[c],
                device_id=member_id(d),
                device_id_type=MESH,
            ).start()

        pltpu.make_async_copy(
            packed.at[c, rest(me)], rows.at[c, rest(me)], own_p.at[c]
        ).start()

    wide_tile = tile_of(gate.shape[1], 256)

    def project(c):
        pltpu.make_async_copy(
            packed.at[c, rest(me)], rows.at[c, rest(me)], own_p.at[c]
        ).wait()
        if early:
            rows[c, part(me, early), :] = packed[c, part(me, early), :]
            arrived(early_but_one(rows.at[c]), early_in_p.at[c])
        arrived(all_but_one(rows.at[c]), in_p.at[c])

        @pl.loop(0, gate.shape[1] // wide_tile)
        def _(j):
            at = part(j, wide_tile)
            gate[:, at] += jnp.dot(
                rows[c], w_gate[part(c, cols), at], preferred_element_type=jnp.float32
            )
            up[:, at] += jnp.dot(
                rows[c], w_up[part(c, cols), at], preferred_element_type=jnp.float32
            )

    @pl.loop(0, LAG)
    def _(c):
        pack(c)

    weights[0].wait()
    weights[1].wait()

    @pl.loop(LAG, chunks)
    def _(c):
        pack(c)
        project(c - LAG)

    weights[2].wait()

    @pl.loop(chunks - LAG, chunks)
    def _(c):
        project(c)

    @pl.loop(0, gate.shape[1] // wide_tile)
    def _(j):
        at = part(j, wide_tile)
        g = gate[:, at] * gate_scale_ref[:, at]
        hidden[:, at] = (g / (1.0 + jnp.exp(-g)) * (up[:, at] * up_scale_ref[:, at])).astype(jnp.bfloat16)

    @pl.loop(0, chunks)
    def _(c):
        @pl.loop(0, cols // half)
        def _(j):
            at = part(c * (cols // half) + j, half)
            results[c, :, part(j, half)] = (
                jnp.dot(hidden[...], w_down[:, at], preferred_element_type=jnp.float32)
                * down_scale_ref[:, at]
            ).astype(jnp.bfloat16)

        @pl.loop(1, members)
        def _(i):
            d = member_at(i)
            pltpu.make_async_remote_copy(
                src_ref=results.at[c, rest(d)],
                dst_ref=returned.at[c, rest(me)],
                send_sem=back_out_p.at[c],
                recv_sem=back_in_p.at[c],
                device_id=member_id(d),
                device_id_type=MESH,
            ).start()

        pltpu.make_async_copy(
            results.at[c, rest(me)], returned.at[c, rest(me)], back_own_p.at[c]
        ).start()

    if early:

        @pl.loop(0, chunks)
        def _(c):
            @pl.loop(1, members)
            def _(i):
                d = member_at(i)
                pltpu.make_async_remote_copy(
                    src_ref=results.at[c, part(d, early)],
                    dst_ref=returned.at[c, part(me, early)],
                    send_sem=late_out_p.at[c],
                    recv_sem=late_in_p.at[c],
                    device_id=member_id(d),
                    device_id_type=MESH,
                ).start()

    @pl.loop(0, chunks)
    def _(c):
        pltpu.make_async_copy(
            results.at[c, rest(me)], returned.at[c, rest(me)], back_own_p.at[c]
        ).wait()
        arrived(all_but_one(returned.at[c]), back_in_p.at[c])

        @pl.loop(0, cols // half)
        def _(j):
            partial[c, pl.ds(away * count, held - away * count), part(j, half)] = jnp.dot(
                combine[pl.ds(away * count, held - away * count), pl.ds(first, members * slots)],
                returned[c, pl.ds(first, members * slots), part(j, half)],
                preferred_element_type=jnp.float32,
            ).astype(jnp.bfloat16)

        @pl.loop(1, groups)
        def _(i):
            pltpu.make_async_remote_copy(
                src_ref=partial.at[c, part(i, count)],
                dst_ref=partials.at[c, part(groups - i, count)],
                send_sem=back_out_z.at[c],
                recv_sem=back_in_z.at[c],
                device_id=group_id(group_at(i)),
                device_id_type=MESH,
            ).start()

    @pl.loop(0, chunks)
    def _(c):
        if early:
            returned[c, part(me, early), :] = results[c, part(me, early), :]
            arrived(early_but_one(returned.at[c]), late_in_p.at[c])
            total = jnp.dot(
                combine[pl.ds(0, count), pl.ds(0, first)],
                returned[c, pl.ds(0, first), :],
                preferred_element_type=jnp.float32,
            )
        else:
            total = partial[c, pl.ds(0, count), :].astype(jnp.float32)
        arrived(partials.at[c, pl.ds(count, (groups - 1) * count)], back_in_z.at[c])
        for g in range(1, groups):
            total += partials[c, pl.ds(g * count, count), :].astype(jnp.float32)
        out_ref[:, part(c, cols)] = total.astype(jnp.bfloat16)

    arrived(metas.at[pl.ds(1, groups - 1)], meta_sems.at[0])

    @pl.loop(0, chunks)
    def _(c):
        if relays:

            @pl.when(is_end)
            def _():
                arrived(tokens.at[c, pl.ds(count, (groups - 2) * count)], out_z.at[c])

            @pl.when(jnp.logical_not(is_end))
            def _():
                arrived(tokens.at[c, pl.ds(count, (groups - 1) * count)], out_z.at[c])
                arrived(tokens.at[c, pl.ds(count, count)], relay_z.at[c])

        else:
            arrived(tokens.at[c, pl.ds(count, (groups - 1) * count)], out_z.at[c])
        if early:
            arrived(early_but_one(packed.at[c]), early_out_p.at[c])
            arrived(early_but_one(results.at[c]), late_out_p.at[c])
        arrived(all_but_one(packed.at[c]), out_p.at[c])
        arrived(all_but_one(results.at[c]), back_out_p.at[c])
        arrived(partial.at[c, pl.ds(count, (groups - 1) * count)], back_out_z.at[c])


def on_device(
    tokens, expert_ids, gate_weights, w_gate, w_up, w_down, gate_scale, up_scale, down_scale
):
    count, top = expert_ids.shape
    width = tokens.shape[1]
    inner = w_gate.shape[2]
    nodes, wides = lax.axis_size("node"), lax.axis_size("wide")
    experts = nodes * wides
    capacity = max(2, 4 * count * top // (3 * experts))
    groups = math.gcd(4, wides)
    ring = wides // groups
    members = nodes * ring
    early = capacity if capacity % 16 == 0 and groups > 1 else 0
    held = groups * count
    chunks = CHUNKS
    cols = width // chunks

    my_group = lax.axis_index("wide") // ring
    named = expert_ids.T[:, None, :] == jnp.arange(experts, dtype=jnp.int32)[None, :, None]
    picked = jnp.any(named, axis=0)
    weight = jnp.sum(jnp.where(named, gate_weights.T[:, None, :], 0.0), axis=0)
    earlier = jnp.arange(count)[:, None] < jnp.arange(count)[None, :]
    position = jnp.dot(
        picked.astype(jnp.bfloat16), earlier.astype(jnp.bfloat16), preferred_element_type=jnp.float32
    )
    distance = (my_group - jnp.arange(groups)) % groups
    here = jnp.arange(held)[None, :] // count == distance[:, None]
    start = (distance * capacity).astype(jnp.float32)

    def tables(values):
        values = values.reshape(nodes, groups, ring, count).transpose(1, 0, 2, 3)
        return jnp.tile(values.reshape(groups, members, count), (1, 1, groups))

    place = jnp.where(picked, position, -float(experts * count))
    place = jnp.where(here[:, None, :], tables(place) + start[:, None, None], -1.0)
    weight = jnp.where(here[:, None, :], tables(weight), 0.0)
    meta = jnp.concatenate([place, weight], axis=1)

    vmem = pl.BlockSpec(memory_space=pltpu.VMEM)
    anywhere = pl.BlockSpec(memory_space=pl.ANY)
    rows = members * groups * capacity
    bf16, f32 = jnp.bfloat16, jnp.float32
    per_chunk = pltpu.SemaphoreType.DMA((chunks,))
    return pl.pallas_call(
        functools.partial(kernel, groups, ring, early),
        out_shape=jax.ShapeDtypeStruct((count, width), bf16),
        in_specs=[vmem, vmem, anywhere, anywhere, anywhere, vmem, vmem, vmem],
        out_specs=vmem,
        scratch_shapes=[
            pltpu.VMEM((groups, 2 * members, held), f32),
            pltpu.VMEM((chunks, held, cols), bf16),
            pltpu.VMEM((chunks, rows, cols), bf16),
            pltpu.VMEM((chunks, rows, cols), bf16),
            pltpu.VMEM((width, inner), bf16),
            pltpu.VMEM((width, inner), bf16),
            pltpu.VMEM((inner, width), bf16),
            pltpu.VMEM((rows, inner), f32),
            pltpu.VMEM((rows, inner), f32),
            pltpu.VMEM((rows, inner), bf16),
            pltpu.VMEM((chunks, rows, cols), bf16),
            pltpu.VMEM((chunks, rows, cols), bf16),
            pltpu.VMEM((chunks, held, cols), bf16),
            pltpu.VMEM((chunks, held, cols), bf16),
            pltpu.VMEM((rows, held), bf16),
            pltpu.VMEM((rows, held), f32),
            pltpu.VMEM((held, rows), bf16),
            pltpu.SemaphoreType.DMA((2,)),
            pltpu.SemaphoreType.DMA((3,)),
        ]
        + [per_chunk] * 17,
        compiler_params=pltpu.CompilerParams(
            collective_id=0, has_side_effects=True, vmem_limit_bytes=60 * 2**20
        ),
    )(tokens, meta, w_gate, w_up, w_down, gate_scale, up_scale, down_scale)


def solution(mesh):
    placed = (
        P(("node", "wide"), None),
        P(("node", "wide"), None),
        P(("node", "wide"), None),
        P(("node", "wide"), None, None),
        P(("node", "wide"), None, None),
        P(("node", "wide"), None, None),
        P(("node", "wide"), None),
        P(("node", "wide"), None),
        P(("node", "wide"), None),
    )
    return jax.shard_map(
        on_device, mesh=mesh, in_specs=placed, out_specs=P(("node", "wide"), None), check_vma=False
    )
```

```python
import functools
import math

import jax
import jax.numpy as jnp
from jax import lax
from jax.experimental import pallas as pl
from jax.experimental.pallas import tpu as pltpu
from jax.sharding import PartitionSpec as P

MESH = pl.DeviceIdType.MESH
CHUNKS = 8
LAG = 1


def tile_of(size, most):
    return most if size % most == 0 else size


def kernel(
    groups,
    ring,
    early,
    tok_ref,
    meta_ref,
    gate_hbm,
    up_hbm,
    down_hbm,
    gate_scale_ref,
    up_scale_ref,
    down_scale_ref,
    out_ref,
    metas,
    tokens,
    packed,
    rows,
    w_gate,
    w_up,
    w_down,
    gate,
    up,
    hidden,
    results,
    returned,
    partial,
    partials,
    relayed,
    dispatch,
    weighted,
    combine,
    meta_sems,
    weight_sems,
    out_z,
    in_z,
    own_z,
    out_p,
    in_p,
    own_p,
    early_out_p,
    early_in_p,
    relay_z,
    back_out_p,
    back_in_p,
    back_own_p,
    late_out_p,
    late_in_p,
    late_own_p,
    back_out_z,
    back_in_z,
    back_relay_z,
):
    chunks, _, cols = tokens.shape
    count = tok_ref.shape[0]
    members = metas.shape[1] // 2
    first = members * early
    slots = packed.shape[1] // members - early
    away = 1 if early else 0
    held = groups * count
    node, wide = lax.axis_index("node"), lax.axis_index("wide")
    my_group, my_ring = lax.div(wide, ring), lax.rem(wide, ring)
    me = node * ring + my_ring

    is_end = jnp.logical_or(my_group == 0, my_group == groups - 1)
    relays = groups == 4

    def group_at(i):
        return lax.rem(my_group + i, groups)

    def group_id(g):
        return (node, g * ring + my_ring)

    def member_at(i):
        return lax.rem(me + i, members)

    def member_id(d):
        return (lax.div(d, ring), my_group * ring + lax.rem(d, ring))

    def part(index, size):
        return pl.ds(pl.multiple_of(index * size, size), size)

    def arrived(ref, sem):
        pltpu.make_async_copy(ref, ref, sem).wait()

    weights = [
        pltpu.make_async_copy(gate_hbm.at[0], w_gate, weight_sems.at[0]),
        pltpu.make_async_copy(up_hbm.at[0], w_up, weight_sems.at[1]),
        pltpu.make_async_copy(down_hbm.at[0], w_down, weight_sems.at[2]),
    ]

    barrier = pltpu.get_barrier_semaphore()

    @pl.loop(1, groups)
    def _(i):
        pl.semaphore_signal(barrier, inc=1, device_id=group_id(group_at(i)), device_id_type=MESH)

    @pl.loop(1, members)
    def _(i):
        pl.semaphore_signal(barrier, inc=1, device_id=member_id(member_at(i)), device_id_type=MESH)

    for w in weights:
        w.start()
    pl.semaphore_wait(barrier, groups + members - 2)

    half = tile_of(cols, 256)

    @pl.loop(1, groups)
    def _(i):
        g = group_at(i)
        pltpu.make_async_remote_copy(
            src_ref=meta_ref.at[g],
            dst_ref=metas.at[groups - i],
            send_sem=meta_sems.at[0],
            recv_sem=meta_sems.at[1],
            device_id=group_id(g),
            device_id_type=MESH,
        ).start()

    @pl.loop(0, chunks)
    def _(c):
        mine = tok_ref.at[:, part(c, cols)]

        @pl.loop(1, groups)
        def _(i):
            g = group_at(i)
            direct = jnp.logical_not(jnp.logical_and(is_end, my_group + g == groups - 1))

            @pl.when(jnp.logical_or(direct, not relays))
            def _():
                pltpu.make_async_remote_copy(
                    src_ref=mine,
                    dst_ref=tokens.at[c, part(groups - i, count)],
                    send_sem=out_z.at[c],
                    recv_sem=in_z.at[c],
                    device_id=group_id(g),
                    device_id_type=MESH,
                ).start()

        pltpu.make_async_copy(mine, tokens.at[c, pl.ds(0, count)], own_z.at[c]).start()

    def fill(place, weight, at, base, size):
        slot = base + lax.broadcasted_iota(jnp.int32, (size, held), 0).astype(jnp.float32)
        for d in range(members):
            same = place[d : d + 1, :] == slot
            dispatch[pl.ds(at + d * size, size), :] = jnp.where(same, 1.0, 0.0).astype(jnp.bfloat16)
            weighted[pl.ds(at + d * size, size), :] = jnp.where(same, weight[d : d + 1, :], 0.0)

    metas[0] = meta_ref[my_group]
    if early:
        fill(metas[0, :members, :], metas[0, members:, :], 0, 0.0, early)

        @pl.loop(0, chunks)
        def _(c):
            @pl.loop(0, cols // half)
            def _(j):
                packed[c, pl.ds(0, first), part(j, half)] = jnp.dot(
                    dispatch[pl.ds(0, first), pl.ds(0, count)],
                    tok_ref[:, part(c * (cols // half) + j, half)],
                    preferred_element_type=jnp.float32,
                ).astype(jnp.bfloat16)

            @pl.loop(1, members)
            def _(i):
                d = member_at(i)
                pltpu.make_async_remote_copy(
                    src_ref=packed.at[c, part(d, early)],
                    dst_ref=rows.at[c, part(me, early)],
                    send_sem=early_out_p.at[c],
                    recv_sem=early_in_p.at[c],
                    device_id=member_id(d),
                    device_id_type=MESH,
                ).start()

    gate[...] = jnp.zeros_like(gate)
    up[...] = jnp.zeros_like(up)

    arrived(metas.at[pl.ds(1, groups - 1)], meta_sems.at[1])
    fill(
        jnp.max(metas[:, :members, :], axis=0),
        jnp.sum(metas[:, members:, :], axis=0),
        first,
        float(early),
        slots,
    )
    combine[...] = weighted[...].T.astype(jnp.bfloat16)

    def rest(d):
        return pl.ds(pl.multiple_of(first + d * slots, early or slots), slots)

    def all_but_one(ref):
        return ref.at[pl.ds(first, (members - 1) * slots)]

    def early_but_one(ref):
        return ref.at[pl.ds(0, (members - 1) * early)]

    def pack(c):
        pltpu.make_async_copy(
            tok_ref.at[:, part(c, cols)], tokens.at[c, pl.ds(0, count)], own_z.at[c]
        ).wait()
        arrived(tokens.at[c, pl.ds(count, (groups - 1) * count)], in_z.at[c])

        if relays:
            @pl.when(jnp.logical_not(is_end))
            def _():
                target = (groups - 1) * (my_group - 1)
                distance = lax.rem(2 * groups - 1 - 2 * target, groups)
                pltpu.make_async_remote_copy(
                    src_ref=tokens.at[c, pl.ds(2 * count, count)],
                    dst_ref=tokens.at[c, part(distance, count)],
                    send_sem=relay_z.at[c],
                    recv_sem=in_z.at[c],
                    device_id=group_id(target),
                    device_id_type=MESH,
                ).start()

        @pl.loop(0, cols // half)
        def _(j):
            packed[c, pl.ds(first, members * slots), part(j, half)] = jnp.dot(
                dispatch[pl.ds(first, members * slots), :],
                tokens[c, :, part(j, half)],
                preferred_element_type=jnp.float32,
            ).astype(jnp.bfloat16)

        @pl.loop(1, members)
        def _(i):
            d = member_at(i)
            pltpu.make_async_remote_copy(
                src_ref=packed.at[c, rest(d)],
                dst_ref=rows.at[c, rest(me)],
                send_sem=out_p.at[c],
                recv_sem=in_p.at[c],
                device_id=member_id(d),
                device_id_type=MESH,
            ).start()

        pltpu.make_async_copy(
            packed.at[c, rest(me)], rows.at[c, rest(me)], own_p.at[c]
        ).start()

    wide_tile = tile_of(gate.shape[1], 256)

    def project(c):
        pltpu.make_async_copy(
            packed.at[c, rest(me)], rows.at[c, rest(me)], own_p.at[c]
        ).wait()
        if early:
            rows[c, part(me, early), :] = packed[c, part(me, early), :]
            arrived(early_but_one(rows.at[c]), early_in_p.at[c])
        arrived(all_but_one(rows.at[c]), in_p.at[c])

        @pl.loop(0, gate.shape[1] // wide_tile)
        def _(j):
            at = part(j, wide_tile)
            gate[:, at] += jnp.dot(
                rows[c], w_gate[part(c, cols), at], preferred_element_type=jnp.float32
            )
            up[:, at] += jnp.dot(
                rows[c], w_up[part(c, cols), at], preferred_element_type=jnp.float32
            )

    @pl.loop(0, LAG)
    def _(c):
        pack(c)

    weights[0].wait()
    weights[1].wait()

    @pl.loop(LAG, chunks)
    def _(c):
        pack(c)
        project(c - LAG)

    weights[2].wait()

    @pl.loop(chunks - LAG, chunks)
    def _(c):
        project(c)

    @pl.loop(0, gate.shape[1] // wide_tile)
    def _(j):
        at = part(j, wide_tile)
        g = gate[:, at] * gate_scale_ref[:, at]
        hidden[:, at] = (g / (1.0 + jnp.exp(-g)) * (up[:, at] * up_scale_ref[:, at])).astype(jnp.bfloat16)

    @pl.loop(0, chunks)
    def _(c):
        @pl.loop(0, cols // half)
        def _(j):
            at = part(c * (cols // half) + j, half)
            results[c, :, part(j, half)] = (
                jnp.dot(hidden[...], w_down[:, at], preferred_element_type=jnp.float32)
                * down_scale_ref[:, at]
            ).astype(jnp.bfloat16)

        @pl.loop(1, members)
        def _(i):
            d = member_at(i)
            pltpu.make_async_remote_copy(
                src_ref=results.at[c, rest(d)],
                dst_ref=returned.at[c, rest(me)],
                send_sem=back_out_p.at[c],
                recv_sem=back_in_p.at[c],
                device_id=member_id(d),
                device_id_type=MESH,
            ).start()

        pltpu.make_async_copy(
            results.at[c, rest(me)], returned.at[c, rest(me)], back_own_p.at[c]
        ).start()

    if early:

        @pl.loop(0, chunks)
        def _(c):
            @pl.loop(1, members)
            def _(i):
                d = member_at(i)
                pltpu.make_async_remote_copy(
                    src_ref=results.at[c, part(d, early)],
                    dst_ref=returned.at[c, part(me, early)],
                    send_sem=late_out_p.at[c],
                    recv_sem=late_in_p.at[c],
                    device_id=member_id(d),
                    device_id_type=MESH,
                ).start()

    def send_back(c, i):
        pltpu.make_async_remote_copy(
            src_ref=partial.at[c, part(i, count)],
            dst_ref=partials.at[c, part(groups - i, count)],
            send_sem=back_out_z.at[c],
            recv_sem=back_in_z.at[c],
            device_id=group_id(group_at(i)),
            device_id_type=MESH,
        ).start()

    def add_and_send(c):
        arrived(relayed.at[c], back_relay_z.at[c])
        mine = partial[c, pl.ds(2 * count, count), :].astype(jnp.float32)
        partial[c, pl.ds(2 * count, count), :] = (
            mine + relayed[c].astype(jnp.float32)
        ).astype(jnp.bfloat16)
        send_back(c, 2)

    @pl.loop(0, chunks)
    def _(c):
        pltpu.make_async_copy(
            results.at[c, rest(me)], returned.at[c, rest(me)], back_own_p.at[c]
        ).wait()
        arrived(all_but_one(returned.at[c]), back_in_p.at[c])

        @pl.loop(0, cols // half)
        def _(j):
            partial[c, pl.ds(away * count, held - away * count), part(j, half)] = jnp.dot(
                combine[pl.ds(away * count, held - away * count), pl.ds(first, members * slots)],
                returned[c, pl.ds(first, members * slots), part(j, half)],
                preferred_element_type=jnp.float32,
            ).astype(jnp.bfloat16)

        @pl.loop(1, groups)
        def _(i):
            g = group_at(i)
            far = jnp.logical_and(is_end, my_group + g == groups - 1)
            later = jnp.logical_and(jnp.logical_not(is_end), i == 2)

            @pl.when(jnp.logical_or(not relays, jnp.logical_not(jnp.logical_or(far, later))))
            def _():
                send_back(c, i)

            if relays:

                @pl.when(far)
                def _():
                    pltpu.make_async_remote_copy(
                        src_ref=partial.at[c, part(i, count)],
                        dst_ref=relayed.at[c],
                        send_sem=back_out_z.at[c],
                        recv_sem=back_relay_z.at[c],
                        device_id=group_id(1 + lax.div(my_group, groups - 1) * (groups - 3)),
                        device_id_type=MESH,
                    ).start()

        if relays:

            @pl.when(jnp.logical_and(jnp.logical_not(is_end), c > 0))
            def _():
                add_and_send(c - 1)

    if relays:

        @pl.when(jnp.logical_not(is_end))
        def _():
            add_and_send(chunks - 1)

    @pl.loop(0, chunks)
    def _(c):
        if early:
            returned[c, part(me, early), :] = results[c, part(me, early), :]
            arrived(early_but_one(returned.at[c]), late_in_p.at[c])
            total = jnp.dot(
                combine[pl.ds(0, count), pl.ds(0, first)],
                returned[c, pl.ds(0, first), :],
                preferred_element_type=jnp.float32,
            )
        else:
            total = partial[c, pl.ds(0, count), :].astype(jnp.float32)
        if relays:

            @pl.when(is_end)
            def _():
                unused = 3 - 2 * lax.div(my_group, groups - 1)
                partials[c, part(unused, count), :] = jnp.zeros((count, cols), jnp.bfloat16)
                arrived(partials.at[c, pl.ds(0, (groups - 2) * count)], back_in_z.at[c])

            @pl.when(jnp.logical_not(is_end))
            def _():
                arrived(partials.at[c, pl.ds(count, (groups - 1) * count)], back_in_z.at[c])

        else:
            arrived(partials.at[c, pl.ds(count, (groups - 1) * count)], back_in_z.at[c])
        for g in range(1, groups):
            total += partials[c, pl.ds(g * count, count), :].astype(jnp.float32)
        out_ref[:, part(c, cols)] = total.astype(jnp.bfloat16)

    arrived(metas.at[pl.ds(1, groups - 1)], meta_sems.at[0])

    @pl.loop(0, chunks)
    def _(c):
        if relays:

            @pl.when(is_end)
            def _():
                arrived(tokens.at[c, pl.ds(count, (groups - 2) * count)], out_z.at[c])

            @pl.when(jnp.logical_not(is_end))
            def _():
                arrived(tokens.at[c, pl.ds(count, (groups - 1) * count)], out_z.at[c])
                arrived(tokens.at[c, pl.ds(count, count)], relay_z.at[c])

        else:
            arrived(tokens.at[c, pl.ds(count, (groups - 1) * count)], out_z.at[c])
        if early:
            arrived(early_but_one(packed.at[c]), early_out_p.at[c])
            arrived(early_but_one(results.at[c]), late_out_p.at[c])
        arrived(all_but_one(packed.at[c]), out_p.at[c])
        arrived(all_but_one(results.at[c]), back_out_p.at[c])
        arrived(partial.at[c, pl.ds(count, (groups - 1) * count)], back_out_z.at[c])


def on_device(
    tokens, expert_ids, gate_weights, w_gate, w_up, w_down, gate_scale, up_scale, down_scale
):
    count, top = expert_ids.shape
    width = tokens.shape[1]
    inner = w_gate.shape[2]
    nodes, wides = lax.axis_size("node"), lax.axis_size("wide")
    experts = nodes * wides
    capacity = max(2, 4 * count * top // (3 * experts))
    groups = math.gcd(4, wides)
    ring = wides // groups
    members = nodes * ring
    early = capacity if capacity % 16 == 0 and groups > 1 else 0
    held = groups * count
    chunks = CHUNKS
    cols = width // chunks

    my_group = lax.axis_index("wide") // ring
    named = expert_ids.T[:, None, :] == jnp.arange(experts, dtype=jnp.int32)[None, :, None]
    picked = jnp.any(named, axis=0)
    weight = jnp.sum(jnp.where(named, gate_weights.T[:, None, :], 0.0), axis=0)
    earlier = jnp.arange(count)[:, None] < jnp.arange(count)[None, :]
    position = jnp.dot(
        picked.astype(jnp.bfloat16), earlier.astype(jnp.bfloat16), preferred_element_type=jnp.float32
    )
    distance = (my_group - jnp.arange(groups)) % groups
    here = jnp.arange(held)[None, :] // count == distance[:, None]
    start = (distance * capacity).astype(jnp.float32)

    def tables(values):
        values = values.reshape(nodes, groups, ring, count).transpose(1, 0, 2, 3)
        return jnp.tile(values.reshape(groups, members, count), (1, 1, groups))

    place = jnp.where(picked, position, -float(experts * count))
    place = jnp.where(here[:, None, :], tables(place) + start[:, None, None], -1.0)
    weight = jnp.where(here[:, None, :], tables(weight), 0.0)
    meta = jnp.concatenate([place, weight], axis=1)

    vmem = pl.BlockSpec(memory_space=pltpu.VMEM)
    anywhere = pl.BlockSpec(memory_space=pl.ANY)
    rows = members * groups * capacity
    bf16, f32 = jnp.bfloat16, jnp.float32
    per_chunk = pltpu.SemaphoreType.DMA((chunks,))
    return pl.pallas_call(
        functools.partial(kernel, groups, ring, early),
        out_shape=jax.ShapeDtypeStruct((count, width), bf16),
        in_specs=[vmem, vmem, anywhere, anywhere, anywhere, vmem, vmem, vmem],
        out_specs=vmem,
        scratch_shapes=[
            pltpu.VMEM((groups, 2 * members, held), f32),
            pltpu.VMEM((chunks, held, cols), bf16),
            pltpu.VMEM((chunks, rows, cols), bf16),
            pltpu.VMEM((chunks, rows, cols), bf16),
            pltpu.VMEM((width, inner), bf16),
            pltpu.VMEM((width, inner), bf16),
            pltpu.VMEM((inner, width), bf16),
            pltpu.VMEM((rows, inner), f32),
            pltpu.VMEM((rows, inner), f32),
            pltpu.VMEM((rows, inner), bf16),
            pltpu.VMEM((chunks, rows, cols), bf16),
            pltpu.VMEM((chunks, rows, cols), bf16),
            pltpu.VMEM((chunks, held, cols), bf16),
            pltpu.VMEM((chunks, held, cols), bf16),
            pltpu.VMEM((chunks, count, cols), bf16),
            pltpu.VMEM((rows, held), bf16),
            pltpu.VMEM((rows, held), f32),
            pltpu.VMEM((held, rows), bf16),
            pltpu.SemaphoreType.DMA((2,)),
            pltpu.SemaphoreType.DMA((3,)),
        ]
        + [per_chunk] * 18,
        compiler_params=pltpu.CompilerParams(
            collective_id=0, has_side_effects=True, vmem_limit_bytes=60 * 2**20
        ),
    )(tokens, meta, w_gate, w_up, w_down, gate_scale, up_scale, down_scale)


def solution(mesh):
    placed = (
        P(("node", "wide"), None),
        P(("node", "wide"), None),
        P(("node", "wide"), None),
        P(("node", "wide"), None, None),
        P(("node", "wide"), None, None),
        P(("node", "wide"), None, None),
        P(("node", "wide"), None),
        P(("node", "wide"), None),
        P(("node", "wide"), None),
    )
    return jax.shard_map(
        on_device, mesh=mesh, in_specs=placed, out_specs=P(("node", "wide"), None), check_vma=False
    )
```
